32 devices in a mesh: dev: 32 (over z, y, x, core).
Axes of the slice: x: 2, y: 2, z: 4, core: 2. Of those that a mesh axis runs over, the one named last changes fastest.
Arguments:
- items: bfloat16 [16384, 1024], P('dev'), may hold values from -6 to 6
- cand_user: int32 [16384, 1], P('dev'), may hold values from 0 to 31; in each aligned block of 512 rows (0 to 511, 512 to 1023, ...) at most 32 rows name the same one
- owner_map: int32 [32], replicated, may hold values from 0 to 31, each once
- hist_blocks: int32 [32], P('dev'), may hold values from 1 to 8
- cache_keys: bfloat16 [32, 1024, 1024], P('dev'), may hold values from -6 to 6
- cache_values: bfloat16 [32, 1024, 1024], P('dev'), may hold values from -6 to 6
- w_in: bfloat16 [1024, 2048], replicated, may hold values from -0.1875 to 0.1875
- w_out: bfloat16 [1024, 1024], replicated, may hold values from -0.1875 to 0.1875
Outputs:
- ranked: bfloat16 [16384, 1024], P('dev')
The draws below stay inside these ranges and needn't reach their ends.
Inputs may be any that keep to these rules, and one draw needn't show every extreme that they name: `cand_user`: the candidates of one device name no user more than 32 times. `owner_map`: each cache slot belongs to exactly one user.
All inputs are finite; a program needn't handle non-finite values.
Results may differ from the reference program's by a relative error of at most 0.0057.
Values may be sent and summed in bfloat16 or wider, within the bound.
No kernel may reach another device: no remote copies, remote signals or barrier semaphores. Data moves between devices by JAX's collectives and lax.ppermute only.
A program may use at most 128 MiB of HBM per device.

```python
import math
import jax
import jax.numpy as jnp
import numpy as np
from jax import lax

D = 1024
HEADS = 8
BLOCK = 128
MAXB = 8
HIST = 1024
CAND_DEV = 512
CAP = 32
USERS = 32
CANDS = 16384
N_DEV = 32


def draw_hist_blocks(key, part):
    first, second = jax.random.split(key)
    lengths = jax.random.randint(first, (USERS,), 1, MAXB + 1)
    order = jax.random.permutation(second, USERS)
    places = jnp.arange(USERS)
    lengths = jnp.where(places == order[0], MAXB, lengths)
    lengths = jnp.where(places == order[1], 1, lengths)
    return lengths.astype(jnp.int32)


def level_of(own_key, extent, pieces, smallest, top_value):
    def one(axis_at, parts):
        draws = jax.random.uniform(jax.random.fold_in(jax.random.fold_in(own_key, 6), axis_at), (parts,), jnp.float32, smallest / len(pieces), top_value / len(pieces))
        return jnp.repeat(jnp.exp(draws), extent[axis_at] // parts).reshape((-1,) + (1,) * (len(extent) - axis_at - 1))

    level = one(*pieces[0])
    for cut in pieces[1:]:
        level = level * one(*cut)
    return level


def assign_block(rng, own, number, rows, count, top, reach, lean):
    ranking = jax.random.permutation(rng, count)
    packed, usual = shares(count, rows * top, reach, lean, True), shares(count, rows * top, reach, lean, False)
    places = jnp.arange(count)

    def named(sizes, rotation):
        used = int((sizes > 0).sum())
        fixed = max(1, used // 4)
        moved = fixed + (places - fixed + rotation * (used - fixed)) % max(1, count - fixed)
        return jnp.zeros((count,), jnp.int32).at[ranking[jnp.where(places < fixed, places, moved)]].set(jnp.asarray(sizes, jnp.int32))

    sizes = jnp.where(number % 4 == 0, named(packed, number // 4), named(usual, number - number // 4 - 1))
    mixed = jax.random.permutation(jax.random.fold_in(own, 3), count)
    giver, receiver = mixed[0:count // 2 * 2:2], mixed[1:count // 2 * 2:2]
    slack = jnp.minimum(sizes[giver] - 1, reach - sizes[receiver]) // 2
    slack = jnp.where((giver == ranking[0]) | (receiver == ranking[0]) | (sizes[receiver] == 0), 0, jnp.maximum(slack, 0))
    moved = jax.random.randint(jax.random.fold_in(own, 4), (count // 2,), 0, 1 << 20) % (slack + 1)
    sizes = sizes.at[giver].add(-moved).at[receiver].add(moved)
    items = jnp.searchsorted(jnp.cumsum(sizes), jnp.arange(rows * top), side="right").astype(jnp.int32)
    table = items.reshape(top, rows).T
    table = table[jax.random.permutation(jax.random.fold_in(own, 1), rows)]
    rotation = jax.random.randint(jax.random.fold_in(own, 2), (rows, 1), 0, top)
    return jnp.take_along_axis(table, (jnp.arange(top)[None, :] + rotation) % top, axis=1)


def shares(amount, total, most, lean, full):
    portions = [(1 << 20) // math.isqrt(rank ** lean) + 1 for rank in range(1, amount + 1)]
    largest = most if full else min(most, max(-(-total // amount), total * portions[0] // sum(portions)))
    least = 1 if total - largest >= amount - 1 else 0
    given, spare = [largest] + [least] * (amount - 1), total - largest - least * (amount - 1)
    while spare > 0:
        movable = [i for i in range(1, amount) if given[i] < largest] or [i for i in range(1, amount) if given[i] < most]
        whole, left = sum([portions[i] for i in movable]), spare
        for i in movable:
            addition = min(most - given[i], max(1, left * portions[i] // whole), spare)
            given[i] = given[i] + addition
            spare = spare - addition
    return np.array(given)


def scatter_about(rng, shape, width, reach, cuts=(), held_as=jnp.bfloat16):
    drawn = width * jax.random.normal(rng, shape, jnp.float32)
    if cuts:
        drawn = drawn * level_of(rng, shape, cuts, -0.22, 0.18)
    return jnp.clip(drawn, -reach, reach).astype(held_as)


def setup_inputs(seed: int = 0) -> dict:
    key_list = jax.random.split(jax.random.key(seed), 9)
    items = scatter_about(key_list[0], (CANDS, D), 1.0, 6.0, ((0, 32),))
    cand_user_keys = jax.random.split(jax.random.fold_in(key_list[1], 1), CANDS // CAND_DEV)
    cand_user_turns = jax.random.permutation(jax.random.fold_in(key_list[1], 3), CANDS // CAND_DEV)
    cand_user = jax.vmap(lambda own, number: assign_block(jax.random.fold_in(key_list[1], 2), own, number, CAND_DEV, USERS, 1, CAP, 2))(cand_user_keys, cand_user_turns).reshape((CANDS, 1))
    owner_map = jax.random.permutation(key_list[2], USERS).astype(jnp.int32)
    hist_blocks = draw_hist_blocks(jax.random.fold_in(key_list[8], 71), 0)
    cache_keys = scatter_about(key_list[4], (USERS, HIST, D), 1.0, 6.0, ((0, 32),))
    cache_values = scatter_about(key_list[5], (USERS, HIST, D), 1.0, 6.0, ((0, 32),))
    w_in = scatter_about(key_list[6], (D, 2 * D), D ** -0.5, 0.1875)
    w_out = scatter_about(key_list[7], (D, D), D ** -0.5, 0.1875)
    return {"items": items, "cand_user": cand_user, "owner_map": owner_map, "hist_blocks": hist_blocks, "cache_keys": cache_keys, "cache_values": cache_values, "w_in": w_in, "w_out": w_out}


def layer_norm(values):
    center = values - lax.optimization_barrier(jnp.mean(values, axis=-1, keepdims=True))
    spread = lax.optimization_barrier(jnp.mean(center * center, axis=-1, keepdims=True))
    return center * lax.rsqrt(spread + 1e-06)

def owner_attention(queries, keys, values, blocks):
    head_dim = D // HEADS
    heads_q = queries.astype(jnp.float32).reshape(-1, HEADS, head_dim)
    key_blocks = keys.astype(jnp.float32).reshape(MAXB, BLOCK, HEADS, head_dim)
    value_blocks = values.astype(jnp.float32).reshape(MAXB, BLOCK, HEADS, head_dim)
    inverse = 1.0 / (BLOCK * blocks).astype(jnp.float32)
    scale = head_dim ** (-0.5)

    def add_block(total, inputs):
        index, key_block, value_block = inputs
        scores = jnp.einsum('rhd,thd->rht', heads_q, key_block) * scale
        live = (index < blocks).astype(jnp.float32)
        weights = (jax.nn.silu(scores) * (inverse * live)).astype(jnp.bfloat16)
        total = total + jnp.einsum('rht,thd->rhd', weights.astype(jnp.float32), value_block)
        return (total, None)
    start = jnp.zeros(heads_q.shape, jnp.float32)
    total, unused = lax.scan(add_block, start, (jnp.arange(MAXB, dtype=jnp.int32), key_blocks, value_blocks))
    return total.reshape(queries.shape).astype(jnp.bfloat16)

def reference(items, cand_user, owner_map, hist_blocks, cache_keys, cache_values, w_in, w_out):
    normed = layer_norm(items.astype(jnp.float32)).astype(jnp.bfloat16)
    active = jax.nn.silu(jnp.dot(normed, w_in, preferred_element_type=jnp.float32))
    gate = active[:, :D].astype(jnp.bfloat16)
    queries = active[:, D:].astype(jnp.bfloat16)
    owner = owner_map[cand_user[:, 0].astype(jnp.int32)].astype(jnp.int32)
    owner_hot = (owner[:, None] == jnp.arange(USERS, dtype=jnp.int32)[None, :]).astype(jnp.int32)
    position = lax.optimization_barrier(jnp.sum((jnp.cumsum(owner_hot, axis=0) - owner_hot) * owner_hot, axis=1)).astype(jnp.int32)
    buffer = jnp.zeros((USERS, N_DEV * CAP, D), jnp.bfloat16).at[owner, position].set(queries)
    attended = lax.map(lambda group: owner_attention(group[0], group[1], group[2], group[3]), (buffer, cache_keys, cache_values, hist_blocks))
    attention = attended[owner, position].astype(jnp.float32)
    mixed_rows = (layer_norm(attention) * gate.astype(jnp.float32)).astype(jnp.bfloat16)
    output = items.astype(jnp.float32) + jnp.dot(mixed_rows, w_out, preferred_element_type=jnp.float32)
    return output.astype(jnp.bfloat16)
```

```python
import functools

import jax
import jax.numpy as jnp
from jax import lax
from jax.experimental import pallas as pl
from jax.experimental.pallas import tpu as pltpu
from jax.sharding import PartitionSpec as P

HEADS = 8
BLOCK = 128
F32 = jnp.float32
BF16 = jnp.bfloat16
VMEM_LIMIT = 40 * 1024 * 1024


def normalize(values):
    center = values - jnp.mean(values, axis=-1, keepdims=True)
    spread = jnp.mean(center * center, axis=-1, keepdims=True)
    return center * lax.rsqrt(spread + 1e-06)


def silu(values):
    half = 0.5 * values
    return half + half * jnp.tanh(half)


def iota(shape, dimension):
    return lax.broadcasted_iota(jnp.int32, shape, dimension)


def dot(left, right):
    return jnp.dot(left, right, preferred_element_type=F32)


def as_row(column):
    rows = column.shape[0]
    return jnp.broadcast_to(column, (rows, 128)).T[0:1, :]


def dispatch_kernel(capacity, items, cand, owner_map, w_query, out, target_out, normed_out, normed, select):
    rows = items.shape[0]
    slots = out.shape[0]
    devices = owner_map.shape[0]

    @pl.when(pl.program_id(0) == 0)
    def _():
        values = normalize(items[...].astype(F32)).astype(BF16)
        normed[...] = values
        normed_out[...] = values
        user_hot = (cand[...] == iota((rows, devices), 1)).astype(F32).astype(BF16)
        to_owner = (owner_map[...] == iota((devices, devices), 1)).astype(F32).astype(BF16)
        owner_hot = dot(user_hot, to_owner)
        before = (iota((rows, rows), 0) > iota((rows, rows), 1)).astype(F32).astype(BF16)
        rank = dot(before, owner_hot.astype(BF16))
        start = (iota((rows, devices), 1) * capacity).astype(F32)
        target = jnp.sum(owner_hot * (rank + start), axis=1, keepdims=True)
        target_out[...] = target.astype(jnp.int32)
        row = as_row(target).astype(jnp.int32)
        select[...] = (iota((slots, rows), 0) == row).astype(F32).astype(BF16)

    query = silu(dot(normed[...], w_query[...])).astype(BF16)
    out[...] = dot(select[...], query).astype(BF16)


def dispatch(items, cand_user, owner_map, w_in, capacity):
    rows, width = items.shape
    devices = owner_map.shape[0]
    tile = 256
    slots = devices * capacity
    whole = lambda i: (0, 0)
    return pl.pallas_call(
        functools.partial(dispatch_kernel, capacity),
        grid=(width // tile,),
        in_specs=[
            pl.BlockSpec((rows, width), whole),
            pl.BlockSpec((rows, 1), whole),
            pl.BlockSpec((devices, 1), whole),
            pl.BlockSpec((width, tile), lambda i: (0, width // tile + i)),
        ],
        out_specs=[
            pl.BlockSpec((slots, tile), lambda i: (0, i)),
            pl.BlockSpec((rows, 1), whole),
            pl.BlockSpec((rows, width), whole),
        ],
        out_shape=[
            jax.ShapeDtypeStruct((slots, width), BF16),
            jax.ShapeDtypeStruct((rows, 1), jnp.int32),
            jax.ShapeDtypeStruct((rows, width), BF16),
        ],
        scratch_shapes=[pltpu.VMEM((rows, width), BF16), pltpu.VMEM((slots, rows), BF16)],
        compiler_params=pltpu.CompilerParams(vmem_limit_bytes=VMEM_LIMIT),
        cost_estimate=pl.CostEstimate(
            flops=2 * rows * width * (width + slots), bytes_accessed=9 << 20, transcendentals=rows * width
        ),
        name="dispatch",
    )(items, cand_user, owner_map.reshape(devices, 1), w_in)


def gate_kernel(normed, w_gate, out):
    out[...] = silu(dot(normed[...], w_gate[...])).astype(BF16)


def gates(normed, w_in):
    rows, width = normed.shape
    tile = 256
    return pl.pallas_call(
        gate_kernel,
        grid=(width // tile,),
        in_specs=[
            pl.BlockSpec((rows, width), lambda i: (0, 0)),
            pl.BlockSpec((width, tile), lambda i: (0, i)),
        ],
        out_specs=pl.BlockSpec((rows, tile), lambda i: (0, i)),
        out_shape=jax.ShapeDtypeStruct((rows, width), BF16),
        compiler_params=pltpu.CompilerParams(vmem_limit_bytes=VMEM_LIMIT),
        cost_estimate=pl.CostEstimate(
            flops=2 * rows * width * width, bytes_accessed=4 << 20, transcendentals=rows * width
        ),
        name="gates",
    )(normed, w_in)


def attend_kernel(blocks, queries, keys, values, out, total):
    rows, head_dim = queries.shape
    tile = min(rows, 256)
    live = blocks[0]
    half_scale = 0.5 * head_dim ** (-0.5)
    total[...] = jnp.zeros_like(total)

    def span(start, size):
        key = keys[pl.ds(start, size), :]
        value = values[pl.ds(start, size), :]
        for first in range(0, rows, tile):
            query = queries[pl.ds(first, tile), :]
            half = half_scale * lax.dot_general(
                query, key, (((1,), (1,)), ((), ())), preferred_element_type=F32
            )
            weight = (half + half * jnp.tanh(half)).astype(BF16)
            total[pl.ds(first, tile), :] += dot(weight, value)

    def pair(index, carry):
        span(pl.multiple_of(index * (2 * BLOCK), 2 * BLOCK), 2 * BLOCK)
        return carry

    lax.fori_loop(0, live // 2, pair, 0)

    @pl.when(live % 2 == 1)
    def _():
        span(pl.multiple_of((live - 1) * BLOCK, BLOCK), BLOCK)

    out[...] = (total[...] * (1.0 / (BLOCK * live).astype(F32))).astype(BF16)


def attend(blocks, queries, keys, values):
    rows, width = queries.shape
    events = keys.shape[0]
    head_dim = width // HEADS
    column = lambda h, blocks: (0, h)
    return pl.pallas_call(
        attend_kernel,
        grid_spec=pltpu.PrefetchScalarGridSpec(
            num_scalar_prefetch=1,
            grid=(HEADS,),
            in_specs=[
                pl.BlockSpec((rows, head_dim), column),
                pl.BlockSpec((events, head_dim), column),
                pl.BlockSpec((events, head_dim), column),
            ],
            out_specs=pl.BlockSpec((rows, head_dim), column),
            scratch_shapes=[pltpu.VMEM((rows, head_dim), F32)],
        ),
        out_shape=jax.ShapeDtypeStruct((rows, width), BF16),
        compiler_params=pltpu.CompilerParams(vmem_limit_bytes=VMEM_LIMIT),
        cost_estimate=pl.CostEstimate(
            flops=4 * rows * width * events, bytes_accessed=8 << 20, transcendentals=rows * HEADS * events
        ),
        name="attend",
    )(blocks, queries, keys, values)


def finish_kernel(target, returned, gate, items, w_out, out):
    rows = items.shape[0]
    slots = returned.shape[0]
    select = (target[...] == iota((rows, slots), 1)).astype(F32).astype(BF16)
    attention = dot(select, returned[...])
    mixed = (normalize(attention) * gate[...].astype(F32)).astype(BF16)
    out[...] = (items[...].astype(F32) + dot(mixed, w_out[...])).astype(BF16)


def finish(target, returned, gate, items, w_out):
    rows, width = items.shape
    slots = returned.shape[0]
    tile = 256
    whole = lambda i: (0, 0)
    part = lambda i: (i, 0)
    return pl.pallas_call(
        finish_kernel,
        grid=(rows // tile,),
        in_specs=[
            pl.BlockSpec((tile, 1), part),
            pl.BlockSpec((slots, width), whole),
            pl.BlockSpec((tile, width), part),
            pl.BlockSpec((tile, width), part),
            pl.BlockSpec((width, width), whole),
        ],
        out_specs=pl.BlockSpec((tile, width), part),
        out_shape=jax.ShapeDtypeStruct((rows, width), BF16),
        compiler_params=pltpu.CompilerParams(vmem_limit_bytes=VMEM_LIMIT),
        cost_estimate=pl.CostEstimate(
            flops=2 * rows * width * (width + slots), bytes_accessed=7 << 20, transcendentals=rows
        ),
        name="finish",
    )(target, returned, gate, items, w_out)


def local(items, cand_user, owner_map, hist_blocks, cache_keys, cache_values, w_in, w_out):
    row_count, width = items.shape
    devices = lax.axis_size("dev")
    capacity = max(2, 2 * row_count // devices)
    outgoing, target, normed = dispatch(items, cand_user, owner_map, w_in, capacity)
    arrived = lax.all_to_all(
        outgoing.reshape(devices, capacity, width), "dev", split_axis=0, concat_axis=0, tiled=True
    )
    gate = gates(normed, w_in)
    attended = attend(hist_blocks, arrived.reshape(-1, width), cache_keys[0], cache_values[0])
    returned = lax.all_to_all(
        attended.reshape(devices, capacity, width), "dev", split_axis=0, concat_axis=0, tiled=True
    )
    return finish(target, returned.reshape(-1, width), gate, items, w_out)


def solution(mesh):
    return jax.shard_map(
        local,
        mesh=mesh,
        in_specs=(
            P("dev", None),
            P("dev", None),
            P(),
            P("dev"),
            P("dev", None, None),
            P("dev", None, None),
            P(),
            P(),
        ),
        out_specs=P("dev", None),
        check_vma=False,
    )
```

```python
import functools

import jax
import jax.numpy as jnp
from jax import lax
from jax.experimental import pallas as pl
from jax.experimental.pallas import tpu as pltpu
from jax.sharding import PartitionSpec as P

HEADS = 8
BLOCK = 128
F32 = jnp.float32
BF16 = jnp.bfloat16
VMEM_LIMIT = 64 * 1024 * 1024 - 64 * 1024
MEMBERS = 8
APART = 2


def normalize(values):
    center = values - jnp.mean(values, axis=-1, keepdims=True)
    spread = jnp.mean(center * center, axis=-1, keepdims=True)
    return center * lax.rsqrt(spread + 1e-06)


def silu(values):
    half = 0.5 * values
    return half + half * jnp.tanh(half)


def iota(shape, dimension):
    return lax.broadcasted_iota(jnp.int32, shape, dimension)


def dot(left, right):
    return jnp.dot(left, right, preferred_element_type=F32)


def exact(condition):
    return condition.astype(F32).astype(BF16)


def params():
    return pltpu.CompilerParams(vmem_limit_bytes=VMEM_LIMIT)


def cost(flops, moved, transcendentals=0):
    return pl.CostEstimate(flops=flops, bytes_accessed=moved, transcendentals=transcendentals)


def as_column(row):
    size = row.shape[1]
    return jnp.broadcast_to(row.astype(F32), (128, size)).T[:, 0:1].astype(jnp.int32)


def route(place, cand, owner_map, capacity):
    rows = cand.shape[1]
    devices = owner_map.shape[1]
    groups = devices // MEMBERS
    user_hot = exact(cand == iota((devices, rows), 0))
    to_owner = exact(owner_map == iota((devices, devices), 0))
    owner_hot = dot(to_owner, user_hot)
    before = exact(iota((rows, rows), 0) < iota((rows, rows), 1))
    rank = dot(owner_hot.astype(BF16), before)
    owner = iota((devices, 128), 0)
    offset = owner ^ place
    group, member = offset // MEMBERS, offset % MEMBERS

    def pick(block):
        start = (block * capacity)[:, 0:1].astype(F32)
        return jnp.sum(owner_hot * (rank + start), axis=0, keepdims=True).astype(jnp.int32)

    return pick(owner), pick(group * MEMBERS + member), pick(member * groups + group)


def prepare_kernel(capacity, place, items, cand, owner_map, w_in, *refs):
    *outs, target_out, back_out, normed, w_query, arrival = refs
    rows, width = items.shape
    part = w_query.shape[1]
    copy = pltpu.make_async_copy(w_in.at[:, pl.ds(width, part)], w_query, arrival)
    copy.start()
    target, ahead, back = route(place[0], cand[...], owner_map[...], capacity)
    target_out[...] = target
    back_out[...] = back
    normed[...] = normalize(items[...].astype(F32)).astype(BF16)
    copy.wait()
    query = silu(dot(normed[...], w_query[...])).astype(BF16)
    size = outs[0].shape[0]
    for index, out in enumerate(outs):
        select = exact(iota((size, rows), 0) + index * size == ahead)
        out[...] = dot(select, query).astype(BF16)


def prepare(place, items, cand_user, owner_map, w_in, capacity, part):
    rows, width = items.shape
    devices = owner_map.shape[0]
    groups = devices // MEMBERS
    slots = devices * capacity
    inside = pl.BlockSpec(memory_space=pltpu.VMEM)
    return pl.pallas_call(
        functools.partial(prepare_kernel, capacity),
        in_specs=[
            pl.BlockSpec(memory_space=pltpu.SMEM),
            inside,
            inside,
            inside,
            pl.BlockSpec(memory_space=pl.ANY),
        ],
        out_specs=[inside] * (groups + 3),
        out_shape=[
            *[jax.ShapeDtypeStruct((slots // groups, part), BF16)] * groups,
            jax.ShapeDtypeStruct((1, rows), jnp.int32),
            jax.ShapeDtypeStruct((1, rows), jnp.int32),
            jax.ShapeDtypeStruct((rows, width), BF16),
        ],
        scratch_shapes=[pltpu.VMEM((width, part), BF16), pltpu.SemaphoreType.DMA],
        compiler_params=params(),
        cost_estimate=cost(2 * rows * part * (width + slots), 4 << 20, rows * part),
        name="prepare",
    )(place, items, cand_user.reshape(1, rows), owner_map.reshape(1, devices), w_in)


def rest_kernel(normed, target, w_in, out, w_query, arrival):
    rows, width = normed.shape
    part = w_query.shape[1]
    copy = pltpu.make_async_copy(w_in.at[:, pl.ds(2 * width - part, part)], w_query, arrival)
    copy.start()
    select = exact(iota((out.shape[0], rows), 0) == target[...])
    copy.wait()
    query = silu(dot(normed[...], w_query[...])).astype(BF16)
    out[...] = dot(select, query).astype(BF16)


def rest(normed, target, w_in, slots, start):
    rows, width = normed.shape
    part = width - start
    inside = pl.BlockSpec(memory_space=pltpu.VMEM)
    return pl.pallas_call(
        rest_kernel,
        in_specs=[inside, inside, pl.BlockSpec(memory_space=pl.ANY)],
        out_specs=inside,
        out_shape=jax.ShapeDtypeStruct((slots, part), BF16),
        scratch_shapes=[pltpu.VMEM((width, part), BF16), pltpu.SemaphoreType.DMA],
        compiler_params=params(),
        cost_estimate=cost(2 * rows * part * (width + slots), 7 << 20, rows * part),
        name="rest",
    )(normed, target, w_in)


def regroup_kernel(count, *refs):
    arrays, outs = refs[:count], refs[count:]
    size = arrays[0].shape[0] // len(outs)
    for first, array in enumerate(arrays):
        for second, out in enumerate(outs):
            out[first * size : (first + 1) * size, :] = array[second * size : (second + 1) * size, :]


def regroup(arrays, parts):
    count = len(arrays)
    rows, width = arrays[0].shape
    size = count * rows // parts
    return pl.pallas_call(
        functools.partial(regroup_kernel, count),
        out_shape=[jax.ShapeDtypeStruct((size, width), BF16)] * parts,
        compiler_params=params(),
        cost_estimate=cost(0, 4 * count * rows * width),
        name="regroup",
    )(*arrays)


def weigh(live, query, keys, values, store):
    half_scale = 0.5 * query.shape[1] ** (-0.5)

    def over(count):
        events = count * BLOCK
        half = half_scale * lax.dot_general(
            query[...], keys[:events, :], (((1,), (1,)), ((), ())), preferred_element_type=F32
        )
        weight = (half + half * jnp.tanh(half)).astype(BF16)
        store((dot(weight, values[:events, :]) * (1.0 / events)).astype(BF16))

    for count in range(1, keys.shape[0] // BLOCK + 1):
        pl.when(live == count)(functools.partial(over, count))


def attend_kernel(blocks, queries, keys, values, out):
    def store(result):
        out[...] = result

    weigh(blocks[0], queries, keys, values, store)


def attend(blocks, queries, keys, values, head):
    rows, width = queries.shape
    events = keys.shape[0]
    head_dim = keys.shape[1] // HEADS
    cache = lambda h, blocks: (0, head + h)
    column = lambda h, blocks: (0, h)
    return pl.pallas_call(
        attend_kernel,
        grid_spec=pltpu.PrefetchScalarGridSpec(
            num_scalar_prefetch=1,
            grid=(width // head_dim,),
            in_specs=[
                pl.BlockSpec((rows, head_dim), column),
                pl.BlockSpec((events, head_dim), cache),
                pl.BlockSpec((events, head_dim), cache),
            ],
            out_specs=pl.BlockSpec((rows, head_dim), column),
        ),
        out_shape=jax.ShapeDtypeStruct((rows, width), BF16),
        compiler_params=params(),
        cost_estimate=cost(8 * rows * width * events, 6 << 20, rows * (width // head_dim) * events),
        name="attend",
    )(blocks, queries, keys, values)


def attend_apart_kernel(members, blocks, *refs):
    queries, (keys, values), outs, gathered = (
        refs[:members],
        refs[members : members + 2],
        refs[members + 2 : -1],
        refs[-1],
    )
    rows = queries[0].shape[0]
    size = rows // len(outs)
    for index, part in enumerate(queries):
        gathered[index * rows : (index + 1) * rows, :] = part[...]

    def store(result):
        for first in range(members):
            for second, out in enumerate(outs):
                start = first * rows + second * size
                out[first * size : (first + 1) * size, :] = result[start : start + size]

    weigh(blocks[0], gathered, keys, values, store)


def attend_apart(blocks, queries, keys, values, groups):
    members = len(queries)
    rows, width = queries[0].shape
    events = keys.shape[0]
    head_dim = keys.shape[1] // HEADS
    column = lambda h, blocks: (0, h)
    out_rows = members * rows // groups
    return pl.pallas_call(
        functools.partial(attend_apart_kernel, members),
        grid_spec=pltpu.PrefetchScalarGridSpec(
            num_scalar_prefetch=1,
            grid=(width // head_dim,),
            in_specs=[
                *[pl.BlockSpec((rows, head_dim), column)] * members,
                pl.BlockSpec((events, head_dim), column),
                pl.BlockSpec((events, head_dim), column),
            ],
            out_specs=[pl.BlockSpec((out_rows, head_dim), column)] * groups,
            scratch_shapes=[pltpu.VMEM((members * rows, head_dim), BF16)],
        ),
        out_shape=[jax.ShapeDtypeStruct((out_rows, width), BF16)] * groups,
        compiler_params=params(),
        cost_estimate=cost(8 * members * rows * width * events, 3 << 20, members * rows * events),
        name="attend_apart",
    )(blocks, *queries, keys, values)


def finish_kernel(members, target, back, returned, *refs):
    apart = refs[:members]
    gate_ref, items_ref, w_ref, out, held, gate, items, weights, arrivals = refs[members:]
    copies = [
        pltpu.make_async_copy(source, kept, arrivals.at[index])
        for index, (source, kept) in enumerate(((w_ref, weights), (gate_ref, gate), (items_ref, items)))
    ]
    for copy in copies:
        copy.start()
    rows = items.shape[0]
    slots = returned.shape[0]
    size = apart[0].shape[0]
    for index, part in enumerate(apart):
        held[index * size : (index + 1) * size, :] = part[...]
    order = iota((rows, slots), 1)
    near = dot(exact(order == as_column(back[...])), held[...])
    far = dot(exact(order == as_column(target[...])), returned[...])
    normed = normalize(jnp.concatenate([near, far], axis=1))
    for copy in copies:
        copy.wait()
    mixed = (normed * gate[...].astype(F32)).astype(BF16)
    out[...] = (items[...].astype(F32) + dot(mixed, weights[...])).astype(BF16)


def finish(target, back, returned, apart, gate, items, w_out):
    rows, width = items.shape
    slots = returned.shape[0]
    anywhere = pl.BlockSpec(memory_space=pl.ANY)
    inside = pl.BlockSpec(memory_space=pltpu.VMEM)
    return pl.pallas_call(
        functools.partial(finish_kernel, len(apart)),
        in_specs=[inside] * (3 + len(apart)) + [anywhere] * 3,
        out_specs=inside,
        out_shape=jax.ShapeDtypeStruct((rows, width), BF16),
        scratch_shapes=[
            pltpu.VMEM((slots, apart[0].shape[1]), BF16),
            pltpu.VMEM((rows, width), BF16),
            pltpu.VMEM((rows, width), BF16),
            pltpu.VMEM((width, width), BF16),
            pltpu.SemaphoreType.DMA((3,)),
        ],
        compiler_params=params(),
        cost_estimate=cost(2 * rows * width * (width + slots), 7 << 20, rows),
        name="finish",
    )(target, back, returned, *apart, gate, items, w_out)


def gate_kernel(normed, w_gate, out):
    out[...] = silu(dot(normed[...], w_gate[...])).astype(BF16)


def gates(normed, w_in):
    rows, width = normed.shape
    tile = 256
    return pl.pallas_call(
        gate_kernel,
        grid=(width // tile,),
        in_specs=[
            pl.BlockSpec((rows, width), lambda i: (0, 0)),
            pl.BlockSpec((width, tile), lambda i: (0, i)),
        ],
        out_specs=pl.BlockSpec((rows, tile), lambda i: (0, i)),
        out_shape=jax.ShapeDtypeStruct((rows, width), BF16),
        compiler_params=params(),
        cost_estimate=pl.CostEstimate(
            flops=2 * rows * width * width, bytes_accessed=4 << 20, transcendentals=rows * width
        ),
        name="gates",
    )(normed, w_in)


def local(items, cand_user, owner_map, hist_blocks, cache_keys, cache_values, w_in, w_out):
    row_count, width = items.shape
    devices = lax.axis_size("dev")
    groups = devices // MEMBERS
    capacity = max(2, 2 * row_count // devices)
    slots = devices * capacity
    part = APART * width // HEADS
    place = lax.axis_index("dev").astype(jnp.int32).reshape(1)
    keys, values = cache_keys[0], cache_values[0]

    def swap(arrays, stride):
        return arrays[:1] + [
            lax.ppermute(array, "dev", [(d, d ^ (index * stride)) for d in range(devices)])
            for index, array in enumerate(arrays)
            if index
        ]

    def exchange(rows):
        blocks = rows.reshape(devices, capacity, rows.shape[1])
        return lax.all_to_all(blocks, "dev", split_axis=0, concat_axis=0, tiled=True).reshape(rows.shape)

    *apart, target, back, normed = prepare(place, items, cand_user, owner_map, w_in, capacity, part)
    apart = swap(apart, MEMBERS)
    outgoing, apart = lax.optimization_barrier((rest(normed, target, w_in, slots, part), apart))
    arrived = exchange(outgoing)
    gate = gates(normed, w_in)
    apart = swap(list(regroup(apart, MEMBERS)), 1)
    apart = list(attend_apart(hist_blocks, apart, keys, values, groups))
    arrived, gate, apart = lax.optimization_barrier((arrived, gate, apart))
    apart = swap(apart, MEMBERS)
    attended, apart = lax.optimization_barrier((attend(hist_blocks, arrived, keys, values, APART), apart))
    returned = exchange(attended)
    apart = swap(list(regroup(apart, MEMBERS)), 1)
    return finish(target, back, returned, apart, gate, items, w_out)


def solution(mesh):
    return jax.shard_map(
        local,
        mesh=mesh,
        in_specs=(
            P("dev", None),
            P("dev", None),
            P(),
            P("dev"),
            P("dev", None, None),
            P("dev", None, None),
            P(),
            P(),
        ),
        out_specs=P("dev", None),
        check_vma=False,
    )
```

```python
import functools

import jax
import jax.numpy as jnp
from jax import lax
from jax.experimental import pallas as pl
from jax.experimental.pallas import tpu as pltpu
from jax.sharding import PartitionSpec as P

HEADS = 8
BLOCK = 128
F32 = jnp.float32
BF16 = jnp.bfloat16
VMEM_LIMIT = 64 * 1024 * 1024 - 64 * 1024
MEMBERS = 8
APART = 3


def normalize(values):
    center = values - jnp.mean(values, axis=-1, keepdims=True)
    spread = jnp.mean(center * center, axis=-1, keepdims=True)
    return center * lax.rsqrt(spread + 1e-06)


def silu(values):
    half = 0.5 * values
    return half + half * jnp.tanh(half)


def iota(shape, dimension):
    return lax.broadcasted_iota(jnp.int32, shape, dimension)


def dot(left, right):
    return jnp.dot(left, right, preferred_element_type=F32)


def exact(condition):
    return condition.astype(F32).astype(BF16)


def params():
    return pltpu.CompilerParams(vmem_limit_bytes=VMEM_LIMIT)


def cost(flops, moved, transcendentals=0):
    return pl.CostEstimate(flops=flops, bytes_accessed=moved, transcendentals=transcendentals)


def as_column(row):
    size = row.shape[1]
    return jnp.broadcast_to(row.astype(F32), (128, size)).T[:, 0:1].astype(jnp.int32)


def route(place, cand, owner_map, capacity):
    rows = cand.shape[1]
    devices = owner_map.shape[1]
    groups = devices // MEMBERS
    user_hot = exact(cand == iota((devices, rows), 0))
    to_owner = exact(owner_map == iota((devices, devices), 0))
    owner_hot = dot(to_owner, user_hot)
    before = exact(iota((rows, rows), 0) < iota((rows, rows), 1))
    rank = dot(owner_hot.astype(BF16), before)
    owner = iota((devices, 128), 0)
    offset = owner ^ place
    group, member = offset // MEMBERS, offset % MEMBERS

    def pick(block):
        start = (block * capacity)[:, 0:1].astype(F32)
        return jnp.sum(owner_hot * (rank + start), axis=0, keepdims=True).astype(jnp.int32)

    return pick(owner), pick(group * MEMBERS + member), pick(member * groups + group)


def started(pairs, arrivals):
    copies = [
        pltpu.make_async_copy(source, kept, arrivals.at[index]) for index, (source, kept) in enumerate(pairs)
    ]
    for copy in copies:
        copy.start()
    return copies


def prepare_kernel(capacity, groups, place, items_in, cand_in, map_in, w_in, *refs):
    outs, slots_out, kept, staged, slots, arrivals, departures = (
        refs[:groups],
        refs[groups],
        refs[groups + 1 : groups + 5],
        refs[-4],
        refs[-3],
        refs[-2],
        refs[-1],
    )
    cand, owner_map, items, w_query = kept
    rows, width = items.shape
    part = w_query.shape[1]
    sources = (cand_in, map_in, items_in, w_in.at[:, pl.ds(width, part)])
    copies = started(zip(sources, kept), arrivals)
    copies[0].wait()
    copies[1].wait()
    target, ahead, back = route(place[0], cand[...], owner_map[...], capacity)
    slots[0:1, :] = target
    slots[1:2, :] = back
    leaving = [pltpu.make_async_copy(slots, slots_out, departures.at[groups])]
    leaving[0].start()
    size = staged.shape[1]
    selects = [exact(iota((size, rows), 0) + index * size == ahead) for index in range(groups)]
    copies[2].wait()
    normed = normalize(items[...].astype(F32)).astype(BF16)
    copies[3].wait()
    query = silu(dot(normed, w_query[...])).astype(BF16)
    for index in range(groups):
        staged[index] = dot(selects[index], query).astype(BF16)
        leaving.append(pltpu.make_async_copy(staged.at[index], outs[index], departures.at[index]))
        leaving[-1].start()
    for copy in leaving:
        copy.wait()


def prepare(place, items, cand_user, owner_map, w_in, capacity, part):
    rows, width = items.shape
    devices = owner_map.shape[0]
    groups = devices // MEMBERS
    size = MEMBERS * capacity
    anywhere = pl.BlockSpec(memory_space=pl.ANY)
    *apart, slots = pl.pallas_call(
        functools.partial(prepare_kernel, capacity, groups),
        in_specs=[pl.BlockSpec(memory_space=pltpu.SMEM)] + [anywhere] * 4,
        out_specs=[anywhere] * (groups + 1),
        out_shape=[
            *[jax.ShapeDtypeStruct((size, part), BF16)] * groups,
            jax.ShapeDtypeStruct((2, rows), jnp.int32),
        ],
        scratch_shapes=[
            pltpu.VMEM((1, rows), jnp.int32),
            pltpu.VMEM((1, devices), jnp.int32),
            pltpu.VMEM((rows, width), BF16),
            pltpu.VMEM((width, part), BF16),
            pltpu.VMEM((groups, size, part), BF16),
            pltpu.VMEM((2, rows), jnp.int32),
            pltpu.SemaphoreType.DMA((4,)),
            pltpu.SemaphoreType.DMA((groups + 1,)),
        ],
        compiler_params=params(),
        cost_estimate=cost(2 * rows * part * (width + groups * size), 4 << 20, rows * part),
        name="prepare",
    )(place, items, cand_user.reshape(1, rows), owner_map.reshape(1, devices), w_in)
    return apart, slots


def rest_kernel(items, slots, w_in, out, w_query, arrival):
    rows, width = items.shape
    part = w_query.shape[1]
    copy = pltpu.make_async_copy(w_in.at[:, pl.ds(2 * width - part, part)], w_query, arrival)
    copy.start()
    select = exact(iota((out.shape[0], rows), 0) == slots[0:1, :])
    normed = normalize(items[...].astype(F32)).astype(BF16)
    copy.wait()
    query = silu(dot(normed, w_query[...])).astype(BF16)
    out[...] = dot(select, query).astype(BF16)


def rest(items, slots, w_in, count, start):
    rows, width = items.shape
    part = width - start
    inside = pl.BlockSpec(memory_space=pltpu.VMEM)
    return pl.pallas_call(
        rest_kernel,
        in_specs=[inside, inside, pl.BlockSpec(memory_space=pl.ANY)],
        out_specs=inside,
        out_shape=jax.ShapeDtypeStruct((count, part), BF16),
        scratch_shapes=[pltpu.VMEM((width, part), BF16), pltpu.SemaphoreType.DMA],
        compiler_params=params(),
        cost_estimate=cost(2 * rows * part * (width + count), 7 << 20, rows * part),
        name="rest",
    )(items, slots, w_in)


def regroup_kernel(count, *refs):
    arrays, outs = refs[:count], refs[count:]
    size = arrays[0].shape[0] // len(outs)
    for first, array in enumerate(arrays):
        for second, out in enumerate(outs):
            out[first * size : (first + 1) * size, :] = array[second * size : (second + 1) * size, :]


def regroup(arrays, parts):
    count = len(arrays)
    rows, width = arrays[0].shape
    size = count * rows // parts
    return pl.pallas_call(
        functools.partial(regroup_kernel, count),
        out_shape=[jax.ShapeDtypeStruct((size, width), BF16)] * parts,
        compiler_params=params(),
        cost_estimate=cost(0, 4 * count * rows * width),
        name="regroup",
    )(*arrays)


def weigh(live, query, keys, values, store):
    half_scale = 0.5 * query.shape[1] ** (-0.5)

    def over(count):
        events = count * BLOCK
        half = half_scale * lax.dot_general(
            query[...], keys[:events, :], (((1,), (1,)), ((), ())), preferred_element_type=F32
        )
        weight = (half + half * jnp.tanh(half)).astype(BF16)
        store((dot(weight, values[:events, :]) * (1.0 / events)).astype(BF16))

    for count in range(1, keys.shape[0] // BLOCK + 1):
        pl.when(live == count)(functools.partial(over, count))


def attend_kernel(blocks, queries, keys, values, out):
    def store(result):
        out[...] = result

    weigh(blocks[0], queries, keys, values, store)


def attend(blocks, queries, keys, values, head):
    rows, width = queries.shape
    events = keys.shape[0]
    head_dim = keys.shape[1] // HEADS
    cache = lambda h, blocks: (0, head + h)
    column = lambda h, blocks: (0, h)
    return pl.pallas_call(
        attend_kernel,
        grid_spec=pltpu.PrefetchScalarGridSpec(
            num_scalar_prefetch=1,
            grid=(width // head_dim,),
            in_specs=[
                pl.BlockSpec((rows, head_dim), column),
                pl.BlockSpec((events, head_dim), cache),
                pl.BlockSpec((events, head_dim), cache),
            ],
            out_specs=pl.BlockSpec((rows, head_dim), column),
        ),
        out_shape=jax.ShapeDtypeStruct((rows, width), BF16),
        compiler_params=params(),
        cost_estimate=cost(8 * rows * width * events, 6 << 20, rows * (width // head_dim) * events),
        name="attend",
    )(blocks, queries, keys, values)


def attend_apart_kernel(members, blocks, *refs):
    queries, (keys, values), outs, gathered = (
        refs[:members],
        refs[members : members + 2],
        refs[members + 2 : -1],
        refs[-1],
    )
    rows = queries[0].shape[0]
    size = rows // len(outs)
    for index, part in enumerate(queries):
        gathered[index * rows : (index + 1) * rows, :] = part[...]

    def store(result):
        for first in range(members):
            for second, out in enumerate(outs):
                start = first * rows + second * size
                out[first * size : (first + 1) * size, :] = result[start : start + size]

    weigh(blocks[0], gathered, keys, values, store)


def attend_apart(blocks, queries, keys, values, groups):
    members = len(queries)
    rows, width = queries[0].shape
    events = keys.shape[0]
    head_dim = keys.shape[1] // HEADS
    column = lambda h, blocks: (0, h)
    out_rows = members * rows // groups
    return pl.pallas_call(
        functools.partial(attend_apart_kernel, members),
        grid_spec=pltpu.PrefetchScalarGridSpec(
            num_scalar_prefetch=1,
            grid=(width // head_dim,),
            in_specs=[
                *[pl.BlockSpec((rows, head_dim), column)] * members,
                pl.BlockSpec((events, head_dim), column),
                pl.BlockSpec((events, head_dim), column),
            ],
            out_specs=[pl.BlockSpec((out_rows, head_dim), column)] * groups,
            scratch_shapes=[pltpu.VMEM((members * rows, head_dim), BF16)],
        ),
        out_shape=[jax.ShapeDtypeStruct((out_rows, width), BF16)] * groups,
        compiler_params=params(),
        cost_estimate=cost(8 * members * rows * width * events, 3 << 20, members * rows * events),
        name="attend_apart",
    )(blocks, *queries, keys, values)


def collect_kernel(members, slots, *refs):
    apart, (out, held) = refs[:members], refs[members:]
    size = apart[0].shape[0]
    for index, part in enumerate(apart):
        held[index * size : (index + 1) * size, :] = part[...]
    select = exact(iota((out.shape[0], held.shape[0]), 1) == as_column(slots[1:2, :]))
    out[...] = dot(select, held[...]).astype(BF16)


def collect(slots, apart):
    rows = slots.shape[1]
    size, width = apart[0].shape
    count = size * len(apart)
    return pl.pallas_call(
        functools.partial(collect_kernel, len(apart)),
        out_shape=jax.ShapeDtypeStruct((rows, width), BF16),
        scratch_shapes=[pltpu.VMEM((count, width), BF16)],
        compiler_params=params(),
        cost_estimate=cost(2 * rows * width * count, 2 << 20),
        name="collect",
    )(slots, *apart)


def finish_kernel(*refs):
    sources, out, kept, (staged, arrivals, departures) = refs[:6], refs[6], refs[7:13], refs[13:]
    slots, returned, near, gate, items, weights = kept
    copies = started(zip(sources, kept), arrivals)
    rows, width = items.shape
    copies[0].wait()
    select = exact(iota((rows, returned.shape[0]), 1) == as_column(slots[0:1, :]))
    copies[1].wait()
    far = dot(select, returned[...])
    copies[2].wait()
    normed = normalize(jnp.concatenate([near[...].astype(F32), far], axis=1))
    for copy in copies[3:]:
        copy.wait()
    mixed = (normed * gate[...].astype(F32)).astype(BF16)
    tile = width // 4
    leaving = []
    for index in range(4):
        part = pl.ds(index * tile, tile)
        staged[:, part] = (items[:, part].astype(F32) + dot(mixed, weights[:, part])).astype(BF16)
        leaving.append(pltpu.make_async_copy(staged.at[:, part], out.at[:, part], departures.at[index]))
        leaving[-1].start()
    for copy in leaving:
        copy.wait()


def finish(slots, returned, near, gate, items, w_out):
    rows, width = items.shape
    count = returned.shape[0]
    anywhere = pl.BlockSpec(memory_space=pl.ANY)
    arrays = (slots, returned, near, gate, items, w_out)
    return pl.pallas_call(
        finish_kernel,
        in_specs=[anywhere] * 6,
        out_specs=anywhere,
        out_shape=jax.ShapeDtypeStruct((rows, width), BF16),
        scratch_shapes=[
            *[pltpu.VMEM(array.shape, array.dtype) for array in arrays],
            pltpu.VMEM((rows, width), BF16),
            pltpu.SemaphoreType.DMA((6,)),
            pltpu.SemaphoreType.DMA((4,)),
        ],
        compiler_params=params(),
        cost_estimate=cost(2 * rows * width * (width + count), 7 << 20, rows),
        name="finish",
    )(*arrays)


def gate_kernel(items, w_in, out, w_gate, arrival):
    width = items.shape[1]
    copy = pltpu.make_async_copy(w_in.at[:, pl.ds(0, width)], w_gate, arrival)
    copy.start()
    normed = normalize(items[...].astype(F32)).astype(BF16)
    copy.wait()
    out[...] = silu(dot(normed, w_gate[...])).astype(BF16)


def gates(items, w_in):
    rows, width = items.shape
    inside = pl.BlockSpec(memory_space=pltpu.VMEM)
    return pl.pallas_call(
        gate_kernel,
        in_specs=[inside, pl.BlockSpec(memory_space=pl.ANY)],
        out_specs=inside,
        out_shape=jax.ShapeDtypeStruct((rows, width), BF16),
        scratch_shapes=[pltpu.VMEM((width, width), BF16), pltpu.SemaphoreType.DMA],
        compiler_params=params(),
        cost_estimate=cost(2 * rows * width * width, 4 << 20, rows * width),
        name="gates",
    )(items, w_in)


def local(items, cand_user, owner_map, hist_blocks, cache_keys, cache_values, w_in, w_out):
    row_count, width = items.shape
    devices = lax.axis_size("dev")
    groups = devices // MEMBERS
    capacity = max(2, 2 * row_count // devices)
    part = APART * width // HEADS
    place = lax.axis_index("dev").astype(jnp.int32).reshape(1)
    keys, values = cache_keys[0], cache_values[0]

    def swap(arrays, stride):
        return arrays[:1] + [
            lax.ppermute(array, "dev", [(d, d ^ (index * stride)) for d in range(devices)])
            for index, array in enumerate(arrays)
            if index
        ]

    def exchange(rows):
        blocks = rows.reshape(devices, capacity, rows.shape[1])
        return lax.all_to_all(blocks, "dev", split_axis=0, concat_axis=0, tiled=True).reshape(rows.shape)

    apart, slots = prepare(place, items, cand_user, owner_map, w_in, capacity, part)
    outgoing, apart = lax.optimization_barrier((rest(items, slots, w_in, devices * capacity, part), swap(apart, MEMBERS)))
    arrived = exchange(outgoing)
    gate = gates(items, w_in)
    apart = swap(list(regroup(apart, MEMBERS)), 1)
    apart = list(attend_apart(hist_blocks, apart, keys, values, groups))
    arrived, gate, apart[0] = lax.optimization_barrier((arrived, gate, apart[0]))
    attended = attend(hist_blocks, arrived, keys, values, APART)
    outgoing, apart = lax.optimization_barrier((attended, swap(apart, MEMBERS)))
    returned = exchange(outgoing)
    apart = swap(list(regroup(apart, MEMBERS)), 1)
    return finish(slots, returned, collect(slots, apart), gate, items, w_out)


def solution(mesh):
    return jax.shard_map(
        local,
        mesh=mesh,
        in_specs=(
            P("dev", None),
            P("dev", None),
            P(),
            P("dev"),
            P("dev", None, None),
            P("dev", None, None),
            P(),
            P(),
        ),
        out_specs=P("dev", None),
        check_vma=False,
    )
```

```python
import functools

import jax
import jax.numpy as jnp
from jax import lax
from jax.experimental import pallas as pl
from jax.experimental.pallas import tpu as pltpu
from jax.sharding import PartitionSpec as P

HEADS = 8
BLOCK = 128
F32 = jnp.float32
BF16 = jnp.bfloat16
VMEM_LIMIT = 64 * 1024 * 1024 - 64 * 1024
MEMBERS = 8
APART = 3


def normalize(values):
    center = values - jnp.mean(values, axis=-1, keepdims=True)
    spread = jnp.mean(center * center, axis=-1, keepdims=True)
    return center * lax.rsqrt(spread + 1e-06)


def silu(values):
    half = 0.5 * values
    return half + half * jnp.tanh(half)


def iota(shape, dimension):
    return lax.broadcasted_iota(jnp.int32, shape, dimension)


def dot(left, right):
    return jnp.dot(left, right, preferred_element_type=F32)


def exact(condition):
    return condition.astype(F32).astype(BF16)


def params():
    return pltpu.CompilerParams(vmem_limit_bytes=VMEM_LIMIT)


def cost(flops, moved, transcendentals=0):
    return pl.CostEstimate(flops=flops, bytes_accessed=moved, transcendentals=transcendentals)


def as_column(row):
    size = row.shape[1]
    return jnp.broadcast_to(row.astype(F32), (128, size)).T[:, 0:1].astype(jnp.int32)


def route(place, cand, owner_map, capacity):
    rows = cand.shape[1]
    devices = owner_map.shape[1]
    groups = devices // MEMBERS
    user_hot = exact(cand == iota((devices, rows), 0))
    to_owner = exact(owner_map == iota((devices, devices), 0))
    owner_hot = dot(to_owner, user_hot)
    before = exact(iota((rows, rows), 0) < iota((rows, rows), 1))
    rank = dot(owner_hot.astype(BF16), before)
    owner = iota((devices, 128), 0)
    offset = owner ^ place
    group, member = (groups - offset // MEMBERS) % groups, offset % MEMBERS

    def pick(block):
        start = (block * capacity)[:, 0:1].astype(F32)
        return jnp.sum(owner_hot * (rank + start), axis=0, keepdims=True).astype(jnp.int32)

    return pick(owner), pick(group * MEMBERS + member), pick(member * groups + group)


def started(pairs, arrivals):
    copies = [
        pltpu.make_async_copy(source, kept, arrivals.at[index]) for index, (source, kept) in enumerate(pairs)
    ]
    for copy in copies:
        copy.start()
    return copies


def prepare_kernel(capacity, groups, place, items_in, cand_in, map_in, w_in, *refs):
    outs, slots_out, kept, staged, slots, arrivals, departures = (
        refs[:groups],
        refs[groups],
        refs[groups + 1 : groups + 5],
        refs[-4],
        refs[-3],
        refs[-2],
        refs[-1],
    )
    cand, owner_map, items, w_query = kept
    rows, width = items.shape
    part = w_query.shape[1]
    sources = (cand_in, map_in, items_in, w_in.at[:, pl.ds(width, part)])
    copies = started(zip(sources, kept), arrivals)
    copies[0].wait()
    copies[1].wait()
    target, ahead, back = route(place[0], cand[...], owner_map[...], capacity)
    slots[0:1, :] = target
    slots[1:2, :] = back
    leaving = [pltpu.make_async_copy(slots, slots_out, departures.at[groups])]
    leaving[0].start()
    size = staged.shape[1]
    selects = [exact(iota((size, rows), 0) + index * size == ahead) for index in range(groups)]
    copies[2].wait()
    normed = normalize(items[...].astype(F32)).astype(BF16)
    copies[3].wait()
    query = silu(dot(normed, w_query[...])).astype(BF16)
    for index in range(groups):
        staged[index] = dot(selects[index], query).astype(BF16)
        leaving.append(pltpu.make_async_copy(staged.at[index], outs[index], departures.at[index]))
        leaving[-1].start()
    for copy in leaving:
        copy.wait()


def prepare(place, items, cand_user, owner_map, w_in, capacity, part):
    rows, width = items.shape
    devices = owner_map.shape[0]
    groups = devices // MEMBERS
    size = MEMBERS * capacity
    anywhere = pl.BlockSpec(memory_space=pl.ANY)
    *apart, slots = pl.pallas_call(
        functools.partial(prepare_kernel, capacity, groups),
        in_specs=[pl.BlockSpec(memory_space=pltpu.SMEM)] + [anywhere] * 4,
        out_specs=[anywhere] * (groups + 1),
        out_shape=[
            *[jax.ShapeDtypeStruct((size, part), BF16)] * groups,
            jax.ShapeDtypeStruct((2, rows), jnp.int32),
        ],
        scratch_shapes=[
            pltpu.VMEM((1, rows), jnp.int32),
            pltpu.VMEM((1, devices), jnp.int32),
            pltpu.VMEM((rows, width), BF16),
            pltpu.VMEM((width, part), BF16),
            pltpu.VMEM((groups, size, part), BF16),
            pltpu.VMEM((2, rows), jnp.int32),
            pltpu.SemaphoreType.DMA((4,)),
            pltpu.SemaphoreType.DMA((groups + 1,)),
        ],
        compiler_params=params(),
        cost_estimate=cost(2 * rows * part * (width + groups * size), 4 << 20, rows * part),
        name="prepare",
    )(place, items, cand_user.reshape(1, rows), owner_map.reshape(1, devices), w_in)
    return apart, slots


def rest_kernel(items, slots, w_in, out, w_query, arrival):
    rows, width = items.shape
    part = w_query.shape[1]
    copy = pltpu.make_async_copy(w_in.at[:, pl.ds(2 * width - part, part)], w_query, arrival)
    copy.start()
    select = exact(iota((out.shape[0], rows), 0) == slots[0:1, :])
    normed = normalize(items[...].astype(F32)).astype(BF16)
    copy.wait()
    query = silu(dot(normed, w_query[...])).astype(BF16)
    out[...] = dot(select, query).astype(BF16)


def rest(items, slots, w_in, count, start):
    rows, width = items.shape
    part = width - start
    inside = pl.BlockSpec(memory_space=pltpu.VMEM)
    return pl.pallas_call(
        rest_kernel,
        in_specs=[inside, inside, pl.BlockSpec(memory_space=pl.ANY)],
        out_specs=inside,
        out_shape=jax.ShapeDtypeStruct((count, part), BF16),
        scratch_shapes=[pltpu.VMEM((width, part), BF16), pltpu.SemaphoreType.DMA],
        compiler_params=params(),
        cost_estimate=cost(2 * rows * part * (width + count), 7 << 20, rows * part),
        name="rest",
    )(items, slots, w_in)


def regroup_kernel(count, *refs):
    arrays, outs = refs[:count], refs[count:]
    size = arrays[0].shape[0] // len(outs)
    for first, array in enumerate(arrays):
        for second, out in enumerate(outs):
            out[first * size : (first + 1) * size, :] = array[second * size : (second + 1) * size, :]


def regroup(arrays, parts):
    count = len(arrays)
    rows, width = arrays[0].shape
    size = count * rows // parts
    return pl.pallas_call(
        functools.partial(regroup_kernel, count),
        out_shape=[jax.ShapeDtypeStruct((size, width), BF16)] * parts,
        compiler_params=params(),
        cost_estimate=cost(0, 4 * count * rows * width),
        name="regroup",
    )(*arrays)


def weigh(live, query, keys, values, store):
    half_scale = 0.5 * query.shape[1] ** (-0.5)

    def over(count):
        events = count * BLOCK
        half = half_scale * lax.dot_general(
            query[...], keys[:events, :], (((1,), (1,)), ((), ())), preferred_element_type=F32
        )
        weight = (half + half * jnp.tanh(half)).astype(BF16)
        store((dot(weight, values[:events, :]) * (1.0 / events)).astype(BF16))

    for count in range(1, keys.shape[0] // BLOCK + 1):
        pl.when(live == count)(functools.partial(over, count))


def attend_kernel(blocks, queries, keys, values, out):
    def store(result):
        out[...] = result

    weigh(blocks[0], queries, keys, values, store)


def attend(blocks, queries, keys, values, head):
    rows, width = queries.shape
    events = keys.shape[0]
    head_dim = keys.shape[1] // HEADS
    cache = lambda h, blocks: (0, head + h)
    column = lambda h, blocks: (0, h)
    return pl.pallas_call(
        attend_kernel,
        grid_spec=pltpu.PrefetchScalarGridSpec(
            num_scalar_prefetch=1,
            grid=(width // head_dim,),
            in_specs=[
                pl.BlockSpec((rows, head_dim), column),
                pl.BlockSpec((events, head_dim), cache),
                pl.BlockSpec((events, head_dim), cache),
            ],
            out_specs=pl.BlockSpec((rows, head_dim), column),
        ),
        out_shape=jax.ShapeDtypeStruct((rows, width), BF16),
        compiler_params=params(),
        cost_estimate=cost(8 * rows * width * events, 6 << 20, rows * (width // head_dim) * events),
        name="attend",
    )(blocks, queries, keys, values)


def attend_apart_kernel(members, blocks, *refs):
    queries, (keys, values), outs, gathered = (
        refs[:members],
        refs[members : members + 2],
        refs[members + 2 : -1],
        refs[-1],
    )
    rows = queries[0].shape[0]
    size = rows // len(outs)
    for index, part in enumerate(queries):
        gathered[index * rows : (index + 1) * rows, :] = part[...]

    def store(result):
        for first in range(members):
            for second, out in enumerate(outs):
                start = first * rows + second * size
                out[first * size : (first + 1) * size, :] = result[start : start + size]

    weigh(blocks[0], gathered, keys, values, store)


def attend_apart(blocks, queries, keys, values, groups):
    members = len(queries)
    rows, width = queries[0].shape
    events = keys.shape[0]
    head_dim = keys.shape[1] // HEADS
    column = lambda h, blocks: (0, h)
    out_rows = members * rows // groups
    return pl.pallas_call(
        functools.partial(attend_apart_kernel, members),
        grid_spec=pltpu.PrefetchScalarGridSpec(
            num_scalar_prefetch=1,
            grid=(width // head_dim,),
            in_specs=[
                *[pl.BlockSpec((rows, head_dim), column)] * members,
                pl.BlockSpec((events, head_dim), column),
                pl.BlockSpec((events, head_dim), column),
            ],
            out_specs=[pl.BlockSpec((out_rows, head_dim), column)] * groups,
            scratch_shapes=[pltpu.VMEM((members * rows, head_dim), BF16)],
        ),
        out_shape=[jax.ShapeDtypeStruct((out_rows, width), BF16)] * groups,
        compiler_params=params(),
        cost_estimate=cost(8 * members * rows * width * events, 3 << 20, members * rows * events),
        name="attend_apart",
    )(blocks, *queries, keys, values)


def collect_kernel(members, slots, *refs):
    apart, (out, held) = refs[:members], refs[members:]
    size = apart[0].shape[0]
    for index, part in enumerate(apart):
        held[index * size : (index + 1) * size, :] = part[...]
    select = exact(iota((out.shape[0], held.shape[0]), 1) == as_column(slots[1:2, :]))
    out[...] = dot(select, held[...]).astype(BF16)


def collect(slots, apart):
    rows = slots.shape[1]
    size, width = apart[0].shape
    count = size * len(apart)
    return pl.pallas_call(
        functools.partial(collect_kernel, len(apart)),
        out_shape=jax.ShapeDtypeStruct((rows, width), BF16),
        scratch_shapes=[pltpu.VMEM((count, width), BF16)],
        compiler_params=params(),
        cost_estimate=cost(2 * rows * width * count, 2 << 20),
        name="collect",
    )(slots, *apart)


def finish_kernel(*refs):
    sources, out, kept, (staged, arrivals, departures) = refs[:6], refs[6], refs[7:13], refs[13:]
    slots, returned, near, gate, items, weights = kept
    copies = started(zip(sources, kept), arrivals)
    rows, width = items.shape
    copies[0].wait()
    select = exact(iota((rows, returned.shape[0]), 1) == as_column(slots[0:1, :]))
    copies[1].wait()
    far = dot(select, returned[...])
    copies[2].wait()
    normed = normalize(jnp.concatenate([near[...].astype(F32), far], axis=1))
    for copy in copies[3:]:
        copy.wait()
    mixed = (normed * gate[...].astype(F32)).astype(BF16)
    tile = width // 4
    leaving = []
    for index in range(4):
        part = pl.ds(index * tile, tile)
        staged[:, part] = (items[:, part].astype(F32) + dot(mixed, weights[:, part])).astype(BF16)
        leaving.append(pltpu.make_async_copy(staged.at[:, part], out.at[:, part], departures.at[index]))
        leaving[-1].start()
    for copy in leaving:
        copy.wait()


def finish(slots, returned, near, gate, items, w_out):
    rows, width = items.shape
    count = returned.shape[0]
    anywhere = pl.BlockSpec(memory_space=pl.ANY)
    arrays = (slots, returned, near, gate, items, w_out)
    return pl.pallas_call(
        finish_kernel,
        in_specs=[anywhere] * 6,
        out_specs=anywhere,
        out_shape=jax.ShapeDtypeStruct((rows, width), BF16),
        scratch_shapes=[
            *[pltpu.VMEM(array.shape, array.dtype) for array in arrays],
            pltpu.VMEM((rows, width), BF16),
            pltpu.SemaphoreType.DMA((6,)),
            pltpu.SemaphoreType.DMA((4,)),
        ],
        compiler_params=params(),
        cost_estimate=cost(2 * rows * width * (width + count), 7 << 20, rows),
        name="finish",
    )(*arrays)


def gate_kernel(items, w_in, out, w_gate, arrival):
    width = items.shape[1]
    copy = pltpu.make_async_copy(w_in.at[:, pl.ds(0, width)], w_gate, arrival)
    copy.start()
    normed = normalize(items[...].astype(F32)).astype(BF16)
    copy.wait()
    out[...] = silu(dot(normed, w_gate[...])).astype(BF16)


def gates(items, w_in):
    rows, width = items.shape
    inside = pl.BlockSpec(memory_space=pltpu.VMEM)
    return pl.pallas_call(
        gate_kernel,
        in_specs=[inside, pl.BlockSpec(memory_space=pl.ANY)],
        out_specs=inside,
        out_shape=jax.ShapeDtypeStruct((rows, width), BF16),
        scratch_shapes=[pltpu.VMEM((width, width), BF16), pltpu.SemaphoreType.DMA],
        compiler_params=params(),
        cost_estimate=cost(2 * rows * width * width, 4 << 20, rows * width),
        name="gates",
    )(items, w_in)


def local(items, cand_user, owner_map, hist_blocks, cache_keys, cache_values, w_in, w_out):
    row_count, width = items.shape
    devices = lax.axis_size("dev")
    groups = devices // MEMBERS
    capacity = max(2, 2 * row_count // devices)
    part = APART * width // HEADS
    place = lax.axis_index("dev").astype(jnp.int32).reshape(1)
    keys, values = cache_keys[0], cache_values[0]

    def swap(arrays, offsets):
        return arrays[:1] + [
            lax.ppermute(array, "dev", [(d, d ^ offset) for d in range(devices)])
            for array, offset in zip(arrays[1:], offsets[1:])
        ]

    across = [(groups - index) % groups * MEMBERS for index in range(groups)]
    within = list(range(MEMBERS))

    def exchange(rows):
        blocks = rows.reshape(devices, capacity, rows.shape[1])
        return lax.all_to_all(blocks, "dev", split_axis=0, concat_axis=0, tiled=True).reshape(rows.shape)

    apart, slots = prepare(place, items, cand_user, owner_map, w_in, capacity, part)
    outgoing, gate, apart = lax.optimization_barrier(
        (rest(items, slots, w_in, devices * capacity, part), gates(items, w_in), swap(apart, across))
    )
    arrived = exchange(outgoing)
    apart = swap(list(regroup(apart, MEMBERS)), within)
    apart = list(attend_apart(hist_blocks, apart, keys, values, groups))
    arrived, gate, apart[0] = lax.optimization_barrier((arrived, gate, apart[0]))
    attended = attend(hist_blocks, arrived, keys, values, APART)
    outgoing, apart = lax.optimization_barrier((attended, swap(apart, across)))
    returned = exchange(outgoing)
    apart = swap(list(regroup(apart, MEMBERS)), within)
    return finish(slots, returned, collect(slots, apart), gate, items, w_out)


def solution(mesh):
    return jax.shard_map(
        local,
        mesh=mesh,
        in_specs=(
            P("dev", None),
            P("dev", None),
            P(),
            P("dev"),
            P("dev", None, None),
            P("dev", None, None),
            P(),
            P(),
        ),
        out_specs=P("dev", None),
        check_vma=False,
    )
```

```python
import functools

import jax
import jax.numpy as jnp
from jax import lax
from jax.experimental import pallas as pl
from jax.experimental.pallas import tpu as pltpu
from jax.sharding import PartitionSpec as P

HEADS = 8
BLOCK = 128
F32 = jnp.float32
BF16 = jnp.bfloat16
VMEM_LIMIT = 64 * 1024 * 1024 - 64 * 1024
MEMBERS = 8
APART = 3


def normalize(values):
    center = values - jnp.mean(values, axis=-1, keepdims=True)
    spread = jnp.mean(center * center, axis=-1, keepdims=True)
    return center * lax.rsqrt(spread + 1e-06)


def silu(values):
    half = 0.5 * values
    return half + half * jnp.tanh(half)


def iota(shape, dimension):
    return lax.broadcasted_iota(jnp.int32, shape, dimension)


def dot(left, right):
    return jnp.dot(left, right, preferred_element_type=F32)


def exact(condition):
    return condition.astype(F32).astype(BF16)


def params():
    return pltpu.CompilerParams(vmem_limit_bytes=VMEM_LIMIT)


def cost(flops, moved, transcendentals=0):
    return pl.CostEstimate(flops=flops, bytes_accessed=moved, transcendentals=transcendentals)


def as_column(row):
    size = row.shape[1]
    return jnp.broadcast_to(row.astype(F32), (128, size)).T[:, 0:1].astype(jnp.int32)


def route(place, cand, owner_map, capacity):
    rows = cand.shape[1]
    devices = owner_map.shape[1]
    groups = devices // MEMBERS
    user_hot = exact(cand == iota((devices, rows), 0))
    to_owner = exact(owner_map == iota((devices, devices), 0))
    owner_hot = dot(to_owner, user_hot)
    before = exact(iota((rows, rows), 0) < iota((rows, rows), 1))
    rank = dot(owner_hot.astype(BF16), before)
    owner = iota((devices, 128), 0)
    offset = owner ^ place
    group, member = (groups - offset // MEMBERS) % groups, offset % MEMBERS

    def pick(block):
        start = (block * capacity)[:, 0:1].astype(F32)
        return jnp.sum(owner_hot * (rank + start), axis=0, keepdims=True).astype(jnp.int32)

    return pick(owner), pick(group * MEMBERS + member), pick(member * groups + group)


def started(pairs, arrivals):
    copies = [
        pltpu.make_async_copy(source, kept, arrivals.at[index]) for index, (source, kept) in enumerate(pairs)
    ]
    for copy in copies:
        copy.start()
    return copies


def prepare_kernel(capacity, groups, place, items_in, cand_in, map_in, w_in, *refs):
    outs, slots_out, kept, staged, slots, arrivals, departures = (
        refs[:groups],
        refs[groups],
        refs[groups + 1 : groups + 5],
        refs[-4],
        refs[-3],
        refs[-2],
        refs[-1],
    )
    cand, owner_map, items, w_query = kept
    rows, width = items.shape
    part = w_query.shape[1]
    sources = (cand_in, map_in, items_in, w_in.at[:, pl.ds(width, part)])
    copies = started(zip(sources, kept), arrivals)
    copies[0].wait()
    copies[1].wait()
    target, ahead, back = route(place[0], cand[...], owner_map[...], capacity)
    slots[0:1, :] = target
    slots[1:2, :] = back
    leaving = [pltpu.make_async_copy(slots, slots_out, departures.at[groups])]
    leaving[0].start()
    size = staged.shape[1]
    selects = [exact(iota((size, rows), 0) + index * size == ahead) for index in range(groups)]
    copies[2].wait()
    normed = normalize(items[...].astype(F32)).astype(BF16)
    copies[3].wait()
    query = silu(dot(normed, w_query[...])).astype(BF16)
    for index in range(groups):
        staged[index] = dot(selects[index], query).astype(BF16)
        leaving.append(pltpu.make_async_copy(staged.at[index], outs[index], departures.at[index]))
        leaving[-1].start()
    for copy in leaving:
        copy.wait()


def prepare(place, items, cand_user, owner_map, w_in, capacity, part):
    rows, width = items.shape
    devices = owner_map.shape[0]
    groups = devices // MEMBERS
    size = MEMBERS * capacity
    anywhere = pl.BlockSpec(memory_space=pl.ANY)
    *apart, slots = pl.pallas_call(
        functools.partial(prepare_kernel, capacity, groups),
        in_specs=[pl.BlockSpec(memory_space=pltpu.SMEM)] + [anywhere] * 4,
        out_specs=[anywhere] * (groups + 1),
        out_shape=[
            *[jax.ShapeDtypeStruct((size, part), BF16)] * groups,
            jax.ShapeDtypeStruct((2, rows), jnp.int32),
        ],
        scratch_shapes=[
            pltpu.VMEM((1, rows), jnp.int32),
            pltpu.VMEM((1, devices), jnp.int32),
            pltpu.VMEM((rows, width), BF16),
            pltpu.VMEM((width, part), BF16),
            pltpu.VMEM((groups, size, part), BF16),
            pltpu.VMEM((2, rows), jnp.int32),
            pltpu.SemaphoreType.DMA((4,)),
            pltpu.SemaphoreType.DMA((groups + 1,)),
        ],
        compiler_params=params(),
        cost_estimate=cost(2 * rows * part * (width + groups * size), 4 << 20, rows * part),
        name="prepare",
    )(place, items, cand_user.reshape(1, rows), owner_map.reshape(1, devices), w_in)
    return apart, slots


def rest_kernel(items, slots, w_in, out, w_query, arrival):
    rows, width = items.shape
    part = w_query.shape[1]
    copy = pltpu.make_async_copy(w_in.at[:, pl.ds(2 * width - part, part)], w_query, arrival)
    copy.start()
    select = exact(iota((out.shape[0], rows), 0) == slots[0:1, :])
    normed = normalize(items[...].astype(F32)).astype(BF16)
    copy.wait()
    query = silu(dot(normed, w_query[...])).astype(BF16)
    out[...] = dot(select, query).astype(BF16)


def rest(items, slots, w_in, count, start):
    rows, width = items.shape
    part = width - start
    inside = pl.BlockSpec(memory_space=pltpu.VMEM)
    return pl.pallas_call(
        rest_kernel,
        in_specs=[inside, inside, pl.BlockSpec(memory_space=pl.ANY)],
        out_specs=inside,
        out_shape=jax.ShapeDtypeStruct((count, part), BF16),
        scratch_shapes=[pltpu.VMEM((width, part), BF16), pltpu.SemaphoreType.DMA],
        compiler_params=params(),
        cost_estimate=cost(2 * rows * part * (width + count), 7 << 20, rows * part),
        name="rest",
    )(items, slots, w_in)


def regroup_kernel(count, parts, *refs):
    arrays, outs, (held, staged, arrivals, departures) = refs[:count], refs[count : count + parts], refs[count + parts :]
    size = held.shape[1] // parts
    copies = started([(array, held.at[index]) for index, array in enumerate(arrays)], arrivals)
    for copy in copies:
        copy.wait()
    leaving = []
    for second in range(parts):
        for first in range(count):
            staged[second, first * size : (first + 1) * size, :] = held[first, second * size : (second + 1) * size, :]
        leaving.append(pltpu.make_async_copy(staged.at[second], outs[second], departures.at[second]))
        leaving[-1].start()
    for copy in leaving:
        copy.wait()


def regroup(arrays, parts):
    count = len(arrays)
    rows, width = arrays[0].shape
    size = count * rows // parts
    anywhere = pl.BlockSpec(memory_space=pl.ANY)
    return pl.pallas_call(
        functools.partial(regroup_kernel, count, parts),
        in_specs=[anywhere] * count,
        out_specs=[anywhere] * parts,
        out_shape=[jax.ShapeDtypeStruct((size, width), BF16)] * parts,
        scratch_shapes=[
            pltpu.VMEM((count, rows, width), BF16),
            pltpu.VMEM((parts, size, width), BF16),
            pltpu.SemaphoreType.DMA((count,)),
            pltpu.SemaphoreType.DMA((parts,)),
        ],
        compiler_params=params(),
        cost_estimate=cost(0, 4 * count * rows * width),
        name="regroup",
    )(*arrays)


def weigh(live, query, keys, values, store):
    half_scale = 0.5 * query.shape[1] ** (-0.5)

    def over(count):
        events = count * BLOCK
        half = half_scale * lax.dot_general(
            query[...], keys[:events, :], (((1,), (1,)), ((), ())), preferred_element_type=F32
        )
        weight = (half + half * jnp.tanh(half)).astype(BF16)
        store((dot(weight, values[:events, :]) * (1.0 / events)).astype(BF16))

    for count in range(1, keys.shape[0] // BLOCK + 1):
        pl.when(live == count)(functools.partial(over, count))


def attend_kernel(blocks, queries, keys, values, out):
    def store(result):
        out[...] = result

    weigh(blocks[0], queries, keys, values, store)


def attend(blocks, queries, keys, values, head):
    rows, width = queries.shape
    events = keys.shape[0]
    head_dim = keys.shape[1] // HEADS
    cache = lambda h, blocks: (0, head + h)
    column = lambda h, blocks: (0, h)
    return pl.pallas_call(
        attend_kernel,
        grid_spec=pltpu.PrefetchScalarGridSpec(
            num_scalar_prefetch=1,
            grid=(width // head_dim,),
            in_specs=[
                pl.BlockSpec((rows, head_dim), column),
                pl.BlockSpec((events, head_dim), cache),
                pl.BlockSpec((events, head_dim), cache),
            ],
            out_specs=pl.BlockSpec((rows, head_dim), column),
        ),
        out_shape=jax.ShapeDtypeStruct((rows, width), BF16),
        compiler_params=params(),
        cost_estimate=cost(8 * rows * width * events, 6 << 20, rows * (width // head_dim) * events),
        name="attend",
    )(blocks, queries, keys, values)


def attend_apart_kernel(members, blocks, *refs):
    queries, (keys, values), outs, gathered = (
        refs[:members],
        refs[members : members + 2],
        refs[members + 2 : -1],
        refs[-1],
    )
    rows = queries[0].shape[0]
    size = rows // len(outs)
    for index, part in enumerate(queries):
        gathered[index * rows : (index + 1) * rows, :] = part[...]

    def store(result):
        for first in range(members):
            for second, out in enumerate(outs):
                start = first * rows + second * size
                out[first * size : (first + 1) * size, :] = result[start : start + size]

    weigh(blocks[0], gathered, keys, values, store)


def attend_apart(blocks, queries, keys, values, groups):
    members = len(queries)
    rows, width = queries[0].shape
    events = keys.shape[0]
    head_dim = keys.shape[1] // HEADS
    column = lambda h, blocks: (0, h)
    out_rows = members * rows // groups
    return pl.pallas_call(
        functools.partial(attend_apart_kernel, members),
        grid_spec=pltpu.PrefetchScalarGridSpec(
            num_scalar_prefetch=1,
            grid=(width // head_dim,),
            in_specs=[
                *[pl.BlockSpec((rows, head_dim), column)] * members,
                pl.BlockSpec((events, head_dim), column),
                pl.BlockSpec((events, head_dim), column),
            ],
            out_specs=[pl.BlockSpec((out_rows, head_dim), column)] * groups,
            scratch_shapes=[pltpu.VMEM((members * rows, head_dim), BF16)],
        ),
        out_shape=[jax.ShapeDtypeStruct((out_rows, width), BF16)] * groups,
        compiler_params=params(),
        cost_estimate=cost(8 * members * rows * width * events, 3 << 20, members * rows * events),
        name="attend_apart",
    )(blocks, *queries, keys, values)


def collect_kernel(members, slots, *refs):
    apart, (out, held) = refs[:members], refs[members:]
    size = apart[0].shape[0]
    for index, part in enumerate(apart):
        held[index * size : (index + 1) * size, :] = part[...]
    select = exact(iota((out.shape[0], held.shape[0]), 1) == as_column(slots[1:2, :]))
    out[...] = dot(select, held[...]).astype(BF16)


def collect(slots, apart):
    rows = slots.shape[1]
    size, width = apart[0].shape
    count = size * len(apart)
    return pl.pallas_call(
        functools.partial(collect_kernel, len(apart)),
        out_shape=jax.ShapeDtypeStruct((rows, width), BF16),
        scratch_shapes=[pltpu.VMEM((count, width), BF16)],
        compiler_params=params(),
        cost_estimate=cost(2 * rows * width * count, 2 << 20),
        name="collect",
    )(slots, *apart)


def finish_kernel(*refs):
    sources, out, kept, (staged, arrivals, departures) = refs[:6], refs[6], refs[7:13], refs[13:]
    slots, returned, near, gate, items, weights = kept
    copies = started(zip(sources, kept), arrivals)
    rows, width = items.shape
    copies[0].wait()
    select = exact(iota((rows, returned.shape[0]), 1) == as_column(slots[0:1, :]))
    copies[1].wait()
    far = dot(select, returned[...])
    copies[2].wait()
    normed = normalize(jnp.concatenate([near[...].astype(F32), far], axis=1))
    for copy in copies[3:]:
        copy.wait()
    mixed = (normed * gate[...].astype(F32)).astype(BF16)
    tile = width // 4
    leaving = []
    for index in range(4):
        part = pl.ds(index * tile, tile)
        staged[:, part] = (items[:, part].astype(F32) + dot(mixed, weights[:, part])).astype(BF16)
        leaving.append(pltpu.make_async_copy(staged.at[:, part], out.at[:, part], departures.at[index]))
        leaving[-1].start()
    for copy in leaving:
        copy.wait()


def finish(slots, returned, near, gate, items, w_out):
    rows, width = items.shape
    count = returned.shape[0]
    anywhere = pl.BlockSpec(memory_space=pl.ANY)
    arrays = (slots, returned, near, gate, items, w_out)
    return pl.pallas_call(
        finish_kernel,
        in_specs=[anywhere] * 6,
        out_specs=anywhere,
        out_shape=jax.ShapeDtypeStruct((rows, width), BF16),
        scratch_shapes=[
            *[pltpu.VMEM(array.shape, array.dtype) for array in arrays],
            pltpu.VMEM((rows, width), BF16),
            pltpu.SemaphoreType.DMA((6,)),
            pltpu.SemaphoreType.DMA((4,)),
        ],
        compiler_params=params(),
        cost_estimate=cost(2 * rows * width * (width + count), 7 << 20, rows),
        name="finish",
    )(*arrays)


def gate_kernel(items, w_in, out, w_gate, arrival):
    width = items.shape[1]
    copy = pltpu.make_async_copy(w_in.at[:, pl.ds(0, width)], w_gate, arrival)
    copy.start()
    normed = normalize(items[...].astype(F32)).astype(BF16)
    copy.wait()
    out[...] = silu(dot(normed, w_gate[...])).astype(BF16)


def gates(items, w_in):
    rows, width = items.shape
    inside = pl.BlockSpec(memory_space=pltpu.VMEM)
    return pl.pallas_call(
        gate_kernel,
        in_specs=[inside, pl.BlockSpec(memory_space=pl.ANY)],
        out_specs=inside,
        out_shape=jax.ShapeDtypeStruct((rows, width), BF16),
        scratch_shapes=[pltpu.VMEM((width, width), BF16), pltpu.SemaphoreType.DMA],
        compiler_params=params(),
        cost_estimate=cost(2 * rows * width * width, 4 << 20, rows * width),
        name="gates",
    )(items, w_in)


def local(items, cand_user, owner_map, hist_blocks, cache_keys, cache_values, w_in, w_out):
    row_count, width = items.shape
    devices = lax.axis_size("dev")
    groups = devices // MEMBERS
    capacity = max(2, 2 * row_count // devices)
    part = APART * width // HEADS
    place = lax.axis_index("dev").astype(jnp.int32).reshape(1)
    keys, values = cache_keys[0], cache_values[0]

    def swap(arrays, offsets):
        return arrays[:1] + [
            lax.ppermute(array, "dev", [(d, d ^ offset) for d in range(devices)])
            for array, offset in zip(arrays[1:], offsets[1:])
        ]

    across = [(groups - index) % groups * MEMBERS for index in range(groups)]
    within = list(range(MEMBERS))

    def exchange(rows):
        blocks = rows.reshape(devices, capacity, rows.shape[1])
        return lax.all_to_all(blocks, "dev", split_axis=0, concat_axis=0, tiled=True).reshape(rows.shape)

    apart, slots = prepare(place, items, cand_user, owner_map, w_in, capacity, part)
    outgoing, gate, apart = lax.optimization_barrier(
        (rest(items, slots, w_in, devices * capacity, part), gates(items, w_in), swap(apart, across))
    )
    arrived = exchange(outgoing)
    apart = swap(list(regroup(apart, MEMBERS)), within)
    apart = list(attend_apart(hist_blocks, apart, keys, values, groups))
    arrived, gate, apart[0] = lax.optimization_barrier((arrived, gate, apart[0]))
    attended = attend(hist_blocks, arrived, keys, values, APART)
    outgoing, apart = lax.optimization_barrier((attended, swap(apart, across)))
    returned = exchange(outgoing)
    apart = swap(list(regroup(apart, MEMBERS)), within)
    return finish(slots, returned, collect(slots, apart), gate, items, w_out)


def solution(mesh):
    return jax.shard_map(
        local,
        mesh=mesh,
        in_specs=(
            P("dev", None),
            P("dev", None),
            P(),
            P("dev"),
            P("dev", None, None),
            P("dev", None, None),
            P(),
            P(),
        ),
        out_specs=P("dev", None),
        check_vma=False,
    )
```
